32 devices in a mesh: parts: 2 (over x), grp: 2 (over core), row: 8 (over z, y).
Axes of the slice: x: 2, y: 2, z: 4, core: 2. Of those that a mesh axis runs over, the one named last changes fastest.
Arguments:
- design: bfloat16 [8192, 1024], P(('parts', 'grp', 'row')), parts along dimension 0, may hold values from -6 to 6
- target: float32 [8192], P(('parts', 'grp', 'row')), parts along dimension 0, may hold values from -6 to 6
- coeffs: bfloat16 [2048], P('parts'), parts along dimension 0, may hold values from -0.1875 to 0.1875
- tau_level: int32 [64], P(('parts', 'grp', 'row')), parts along dimension 0, may hold values from 0 to 3
- bucket: int32 [8192], P(('parts', 'grp', 'row')), parts along dimension 0, may hold values from 0 to 63
- sign_bit: int32 [8192], P(('parts', 'grp', 'row')), parts along dimension 0, may hold values from 0 to 1
- panel_order: int32 [16], P('parts'), parts along dimension 0, may hold values from 0 to 7, each once
Outputs:
- rotated: float32 [2048, 1024], P(('parts', 'grp'), 'row'), parts along dimension 0
The draws below stay inside these ranges and needn't reach their ends.
There are 2 independent parts, one for each index of `parts`. The reference program is written for one: setup_inputs(seed, part) draws one part's arguments, and reference() takes and returns one part's arrays. A program takes and returns all parts, laid end to end along the dimension named above; each array names one. Nothing has to cross between parts.
Inputs may be any that keep to these rules, and one draw needn't show every extreme that they name: `panel_order`: each of 0 to 7 once.
All inputs are finite; a program needn't handle non-finite values. Where the reference program divides by a largest or mean magnitude, that divisor is 1e-20 or more.
Results may differ from the reference program's by a relative error of at most 0.0044.
Values may be sent and summed in bfloat16 or wider, within the bound.
A program may use at most 64 MiB of HBM per device.

```python
import jax
import jax.numpy as jnp
import numpy as np
from jax import lax

PANEL = 128
N = 1024
PANELS = 8
ROW_DEV = 256
KB = 64
M = 4096
K = 1024
BLOCK = 128
ROUNDS = 5
NS_ITERS = 4


def plant(drawn, rng, least, largest):
    extent = drawn.shape
    place = [jax.random.randint(jax.random.fold_in(rng, axis), (), 0, extent[axis]) for axis in range(len(extent))]
    drawn = drawn.at[tuple(place)].set(least)
    longest = extent.index(max(extent))
    place[longest] = (place[longest] + 1) % extent[longest]
    return drawn.at[tuple(place)].set(largest)


def steps_of(own_key, extent, cuts, low, largest):
    gain = 1.0
    for axis_at, shards_of in cuts:
        draws = jax.random.uniform(jax.random.fold_in(jax.random.fold_in(own_key, 6), axis_at), (shards_of,), jnp.float32, low / len(cuts), largest / len(cuts))
        gain = gain * jnp.repeat(jnp.exp(draws), extent[axis_at] // shards_of).reshape((-1,) + (1,) * (len(extent) - 1 - axis_at))
    return gain


def noise(own_key, dims, deviation, limit, shards=(), kind=jnp.bfloat16):
    array = deviation * jax.random.normal(own_key, dims, jnp.float32)
    if shards:
        array = array * steps_of(own_key, dims, shards, -0.22, 0.18)
    return jnp.clip(array, -limit, limit).astype(kind)


def setup_inputs(seed: int = 0, part: int = 0) -> dict:
    seeds = jax.random.split(jax.random.key(seed), 8)
    own_keys = jax.random.split(jax.random.fold_in(seeds[7], part), 8)
    return {
        "design": noise(own_keys[0], (M, N), 1.0, 6.0, ((0, 16),)),
        "target": noise(own_keys[1], (M,), 1.0, 6.0, ((0, 16),), jnp.float32),
        "coeffs": noise(own_keys[2], (N,), N ** -0.5, 0.1875),
        "tau_level": plant(jax.random.randint(own_keys[3], (M // BLOCK,), 0, 4), jax.random.fold_in(own_keys[3], 1), 0, 3).astype(jnp.int32),
        "bucket": plant(jax.random.randint(own_keys[4], (M,), 0, KB), jax.random.fold_in(own_keys[4], 1), 0, KB - 1).astype(jnp.int32),
        "sign_bit": plant(jax.random.randint(own_keys[5], (M,), 0, 2), jax.random.fold_in(own_keys[5], 1), 0, 1).astype(jnp.int32),
        "panel_order": jax.random.permutation(own_keys[6], PANELS).astype(jnp.int32),
    }


def sketch_block(design, target, coeffs, tau_level, bucket, sign_bit):
    rows = design.shape[0]
    fitted = jnp.dot(design, coeffs, preferred_element_type=jnp.float32)
    residual = target - fitted
    blocks = tau_level.shape[0]
    quantile = 0.1 + 0.25 * tau_level.astype(jnp.float32)
    quantile = jnp.broadcast_to(quantile[:, None], (blocks, rows // blocks)).reshape(rows)
    upper = jax.nn.sigmoid(residual / 0.2)
    weight = (quantile * upper + (1.0 - quantile) * (1.0 - upper)) / jnp.sqrt(residual * residual + 0.25)
    signed = ((2.0 * sign_bit.astype(jnp.float32) - 1.0) * jnp.sqrt(weight)).astype(jnp.bfloat16)
    slots = lax.broadcasted_iota(jnp.int32, (KB, rows), 0)
    embed = jnp.where(slots == bucket[None, :], signed[None, :], jnp.zeros((), jnp.bfloat16))
    return jnp.dot(embed, design, preferred_element_type=jnp.float32).astype(jnp.bfloat16)

def pair_transform(gram):
    squares = jnp.diagonal(gram)
    inv_root = lax.rsqrt(squares)
    normed = gram * inv_root[:, None] * inv_root[None, :]
    bound = jnp.max(lax.optimization_barrier(jnp.sum(jnp.abs(normed), axis=1)))
    identity = jnp.eye(gram.shape[0], dtype=jnp.float32)
    current = normed / bound
    inverse = identity
    for iteration in range(NS_ITERS):
        middle = 1.5 * identity - 0.5 * jnp.dot(inverse, current, precision=lax.Precision.HIGHEST)
        current_next = jnp.dot(current, middle, precision=lax.Precision.HIGHEST)
        inverse = jnp.dot(middle, inverse, precision=lax.Precision.HIGHEST)
        current = current_next
    return inv_root[:, None] * inverse * (jnp.sqrt(squares) / jnp.sqrt(bound))[None, :]

def reference(design, target, coeffs, tau_level, bucket, sign_bit, panel_order):
    groups = design.shape[0] // ROW_DEV

    def one_block(pieces):
        block_design, block_target, block_level, block_bucket, block_sign = pieces
        return sketch_block(block_design, block_target, coeffs, block_level, block_bucket, block_sign)
    sketch = lax.map(one_block, (design.reshape(groups, ROW_DEV, N), target.reshape(groups, ROW_DEV), tau_level.reshape(groups, ROW_DEV // BLOCK), bucket.reshape(groups, ROW_DEV), sign_bit.reshape(groups, ROW_DEV)))
    sketch = sketch.reshape(K, PANELS, PANEL)
    panels = jnp.take(sketch, panel_order, axis=1).astype(jnp.float32)
    depth = PANELS.bit_length() - 1
    positions = np.arange(PANELS)
    for turn in range(ROUNDS):
        bit = turn % depth
        lows = positions[positions >> bit & 1 == 0]
        highs = lows + (1 << bit)
        pairs = jnp.concatenate([panels[:, lows, :], panels[:, highs, :]], axis=2)
        gram = jnp.einsum('kpa,kpb->pab', pairs, pairs, precision=lax.Precision.HIGHEST)
        mixing = jax.vmap(pair_transform)(gram)
        updated = jnp.einsum('kpa,pab->kpb', pairs, mixing, precision=lax.Precision.HIGHEST)
        panels = panels.at[:, lows, :].set(updated[:, :, :PANEL])
        panels = panels.at[:, highs, :].set(updated[:, :, PANEL:])
    return panels.reshape(K, N)
```

```python
import functools

import jax
import jax.numpy as jnp
from jax import lax
from jax.experimental import pallas as pl
from jax.experimental.pallas import tpu as pltpu
from jax.sharding import PartitionSpec as P

PANEL = 128
KB = 64
ROUNDS = 5
NS_ITERS = 4
CHUNKS = 2
MESH = pl.DeviceIdType.MESH
F32 = jnp.float32
BF16 = jnp.bfloat16


def dot(left, right):
    return jnp.dot(left, right, preferred_element_type=F32)


def cross(left, right):
    return lax.dot_general(left, right, (((0,), (0,)), ((), ())), preferred_element_type=F32)


def split(value):
    high = value.astype(BF16)
    return high, (value - high.astype(F32)).astype(BF16)


def product(left, right):
    return dot(left[0], right[0]) + (dot(left[0], right[1]) + dot(left[1], right[0]))


def stacked(upper, lower):
    return tuple(jnp.concatenate(pair, axis=0) for pair in zip(upper, lower))


def transform_columns(gram, width):
    size = gram.shape[0]
    same = lax.broadcasted_iota(jnp.int32, gram.shape, 0) == lax.broadcasted_iota(
        jnp.int32, gram.shape, 1
    )
    diagonal = jnp.where(same, gram, 0.0)
    squares_row = jnp.sum(diagonal, axis=0, keepdims=True)
    squares_col = jnp.sum(diagonal, axis=1, keepdims=True)
    inv_row = lax.rsqrt(squares_row)
    inv_col = lax.rsqrt(squares_col)
    normed = gram * inv_col * inv_row
    bound = jnp.max(jnp.sum(jnp.abs(normed), axis=0, keepdims=True), axis=1, keepdims=True)
    current = normed / bound

    def middle_of(value):
        return jnp.where(same, 1.5, 0.0) - 0.5 * value

    middle = split(middle_of(current))
    inverse = middle
    current = split(product(split(current), middle))
    for iteration in range(1, NS_ITERS):
        middle = split(middle_of(product(inverse, current)))
        if iteration < NS_ITERS - 1:
            both = product(stacked(current, inverse), middle)
            current = split(both[:size])
            inverse = split(both[size:])
    inverse = product(middle, tuple(part[:, :width] for part in inverse))
    return inv_col * inverse * (jnp.sqrt(squares_row[:, :width]) / jnp.sqrt(bound))


def kernel(
    count,
    design_ref, target_ref, coeffs_ref, tau_ref, bucket_ref, sign_ref, order_ref,
    out_ref,
    piece, own, owned, partner, mine_self, mine_other, their_self, their_other,
    deal_send, deal_recv, pass_send, pass_recv, swap_send, swap_recv, gram_send, gram_recv,
):
    me = lax.axis_index("row")
    sibling = {"grp": 1 - lax.axis_index("grp")}
    depth = count.bit_length() - 1
    half = count * KB
    chunk = half // CHUNKS

    def paired(turn):
        step = 1 << (turn % depth)
        return {"row": me + step * (1 - 2 * ((me // step) % 2))}

    def remote(source, target, send, recv, device):
        return pltpu.make_async_remote_copy(
            src_ref=source, dst_ref=target, send_sem=send, recv_sem=recv,
            device_id=device, device_id_type=MESH,
        )

    barrier = pltpu.get_barrier_semaphore()
    for away in range(1, count):
        pl.semaphore_signal(
            barrier, inc=1, device_id={"row": lax.rem(me + away, count)}, device_id_type=MESH
        )
    pl.semaphore_signal(barrier, inc=1, device_id=sibling, device_id_type=MESH)

    rows = design_ref.shape[0]
    fitted = lax.dot_general(
        jnp.broadcast_to(coeffs_ref[...], (16, coeffs_ref.shape[1])),
        design_ref[...],
        (((1,), (1,)), ((), ())),
        preferred_element_type=F32,
    )[:1]
    residual = target_ref[...] - fitted
    blocks = tau_ref.shape[0]
    lane = lax.broadcasted_iota(jnp.int32, (1, rows), 1)
    level = jnp.zeros((1, rows), F32)
    for block in range(blocks):
        first = block * (rows // blocks)
        level = jnp.where(lane >= first, tau_ref[block].astype(F32), level)
    quantile = 0.1 + 0.25 * level
    upper = jax.nn.sigmoid(residual / 0.2)
    weight = (quantile * upper + (1.0 - quantile) * (1.0 - upper)) / jnp.sqrt(
        residual * residual + 0.25
    )
    signed = (2.0 * sign_ref[...].astype(F32) - 1.0) * jnp.sqrt(weight)
    slots = lax.broadcasted_iota(jnp.int32, (KB, rows), 0)
    embed = jnp.where(slots == bucket_ref[...], signed, 0.0).astype(BF16)

    sketch = dot(embed, design_ref[...])

    def sketch_of(position):
        wanted = jnp.full((KB, PANEL), order_ref[position], jnp.int32)
        chosen = sketch[:, :PANEL]
        for panel in range(1, count):
            chosen = jnp.where(
                wanted == panel, sketch[:, panel * PANEL : (panel + 1) * PANEL], chosen
            )
        return chosen.astype(BF16)

    def rows_of(source):
        return pl.ds(pl.multiple_of(source * KB, KB), KB)

    pl.semaphore_wait(barrier, count)

    def deal(away, position):
        return remote(
            piece.at[away], owned.at[0, rows_of(me)], deal_send.at[away], deal_recv.at[me],
            {"row": position},
        )

    for away in range(1, count):
        position = lax.rem(me + away, count)
        piece[away] = sketch_of(position)
        deal(away, position).start()
    owned[0, rows_of(me), :] = sketch_of(me)

    def passed(source):
        return remote(
            owned.at[0, rows_of(source)], partner.at[0, rows_of(source)],
            pass_send.at[source], pass_recv.at[source], paired(0),
        )

    passed(me).start()
    for away in range(1, count):
        source = lax.rem(me + count - away, count)
        remote(
            piece.at[away], owned.at[0, rows_of(source)], deal_send.at[away],
            deal_recv.at[source], {"row": source},
        ).wait_recv()
        passed(source).start()

    def swap(turn, index):
        part = pl.ds(index * chunk, chunk)
        return remote(
            owned.at[turn, part], partner.at[turn, part],
            swap_send.at[turn, index], swap_recv.at[turn, index], paired(turn),
        )

    def self_copy(turn):
        return remote(
            mine_self.at[turn], their_self.at[turn], gram_send.at[turn, 0],
            gram_recv.at[turn, 0], sibling,
        )

    def other_copy(turn):
        return remote(
            mine_other.at[turn], their_other.at[turn], gram_send.at[turn, 1],
            gram_recv.at[turn, 1], sibling,
        )

    for turn in range(ROUNDS):
        held = owned[turn]
        mine_self[turn] = cross(held, held)
        self_copy(turn).start()
        if turn == 0:
            for source in range(count):
                passed(source).wait_recv()
        else:
            for index in range(CHUNKS):
                swap(turn, index).wait_recv()
        both = jnp.concatenate([held, partner[turn]], axis=1)
        mine_other[turn] = cross(partner[turn], both)
        other_copy(turn).start()
        self_copy(turn).wait_recv()
        self_gram = mine_self[turn] + their_self[turn]
        other_copy(turn).wait_recv()
        other_gram = mine_other[turn] + their_other[turn]
        gram = jnp.concatenate(
            [
                jnp.concatenate([self_gram, other_gram[:, :PANEL].T], axis=1),
                other_gram,
            ],
            axis=0,
        )
        high, low = split(transform_columns(gram, PANEL))
        mixing = jnp.concatenate([high, low], axis=1)
        for index in range(CHUNKS):
            part = pl.ds(index * chunk, chunk)
            bulk = dot(
                jnp.concatenate([owned[turn, part, :], partner[turn, part, :]], axis=1), mixing
            )
            fresh = bulk[:, :PANEL] + bulk[:, PANEL:]
            if turn > 0:
                rest = (own[part, :] - owned[turn, part, :].astype(F32)).astype(BF16)
                fresh = fresh + dot(rest, high[:PANEL])
            if turn < ROUNDS - 1:
                own[part, :] = fresh
                owned[turn + 1, part, :] = fresh.astype(BF16)
                swap(turn + 1, index).start()
            else:
                out_ref[part, :] = fresh

    for away in range(1, count):
        deal(away, lax.rem(me + away, count)).wait_send()
    for source in range(count):
        passed(source).wait_send()
    for turn in range(ROUNDS):
        self_copy(turn).wait_send()
        other_copy(turn).wait_send()
        if turn > 0:
            for index in range(CHUNKS):
                swap(turn, index).wait_send()


def per_device(count, design, target, coeffs, tau_level, bucket, sign_bit, panel_order):
    half = count * KB
    vmem = pl.BlockSpec(memory_space=pltpu.VMEM)
    smem = pl.BlockSpec(memory_space=pltpu.SMEM)
    dma = pltpu.SemaphoreType.DMA
    return pl.pallas_call(
        functools.partial(kernel, count),
        out_shape=jax.ShapeDtypeStruct((half, PANEL), F32),
        in_specs=[vmem, vmem, vmem, smem, vmem, vmem, smem],
        out_specs=vmem,
        scratch_shapes=[
            pltpu.VMEM((count, KB, PANEL), BF16),
            pltpu.VMEM((half, PANEL), F32),
            pltpu.VMEM((ROUNDS, half, PANEL), BF16),
            pltpu.VMEM((ROUNDS, half, PANEL), BF16),
            pltpu.VMEM((ROUNDS, PANEL, PANEL), F32),
            pltpu.VMEM((ROUNDS, PANEL, 2 * PANEL), F32),
            pltpu.VMEM((ROUNDS, PANEL, PANEL), F32),
            pltpu.VMEM((ROUNDS, PANEL, 2 * PANEL), F32),
            dma((count,)), dma((count,)), dma((count,)), dma((count,)),
            dma((ROUNDS, CHUNKS)), dma((ROUNDS, CHUNKS)), dma((ROUNDS, 2)), dma((ROUNDS, 2)),
        ],
        compiler_params=pltpu.CompilerParams(
            collective_id=0, has_side_effects=True, vmem_limit_bytes=48 * 2**20
        ),
    )(
        design, target.reshape(1, -1), coeffs.reshape(1, -1), tau_level,
        bucket.reshape(1, -1), sign_bit.reshape(1, -1), panel_order,
    )


def solution(mesh):
    placed = (
        P(("parts", "grp", "row"), None),
        P(("parts", "grp", "row")),
        P("parts"),
        P(("parts", "grp", "row")),
        P(("parts", "grp", "row")),
        P(("parts", "grp", "row")),
        P("parts"),
    )
    return jax.shard_map(
        functools.partial(per_device, mesh.shape["row"]),
        mesh=mesh,
        in_specs=placed,
        out_specs=P(("parts", "grp"), "row"),
        check_vma=False,
    )
```

```python
import functools

import jax
import jax.numpy as jnp
from jax import lax
from jax.experimental import pallas as pl
from jax.experimental.pallas import tpu as pltpu
from jax.sharding import PartitionSpec as P

PANEL = 128
KB = 64
ROUNDS = 5
NS_ITERS = 4
CHUNKS = 2
MESH = pl.DeviceIdType.MESH
F32 = jnp.float32
BF16 = jnp.bfloat16


def dot(left, right):
    return jnp.dot(left, right, preferred_element_type=F32)


def cross(left, right):
    return lax.dot_general(left, right, (((0,), (0,)), ((), ())), preferred_element_type=F32)


def shifted(scale, rest):
    return scale, rest, rest.astype(BF16)


def mixed(left, right, square):
    return shifted(left[0] * right[0], right[0] * left[1] + left[0] * right[1] + square)


def product(left, right):
    return mixed(left, right, dot(left[2], right[2]))


def middle_of(value):
    return shifted(1.5 - 0.5 * value[0], -0.5 * value[1])


def transform_columns(gram, width):
    size = gram.shape[0]
    same = lax.broadcasted_iota(jnp.int32, gram.shape, 0) == lax.broadcasted_iota(
        jnp.int32, gram.shape, 1
    )
    diagonal = jnp.where(same, gram, 0.0)
    squares_row = jnp.sum(diagonal, axis=0, keepdims=True)
    squares_col = jnp.sum(diagonal, axis=1, keepdims=True)
    inv_row = lax.rsqrt(squares_row)
    inv_col = lax.rsqrt(squares_col)
    normed = gram * inv_col * inv_row
    bound = jnp.max(jnp.sum(jnp.abs(normed), axis=0, keepdims=True), axis=1, keepdims=True)
    share = 1.0 / bound
    current = shifted(share, normed * share - jnp.where(same, share, 0.0))
    middle = middle_of(current)
    inverse = middle
    current = product(current, middle)
    for iteration in range(1, NS_ITERS):
        middle = middle_of(product(inverse, current))
        if iteration < NS_ITERS - 1:
            squares = dot(jnp.concatenate([current[2], inverse[2]], axis=0), middle[2])
            current = mixed(current, middle, squares[:size])
            inverse = mixed(inverse, middle, squares[size:])
    inverse = tuple([inverse[0]] + [part[:, :width] for part in inverse[1:]])
    square = dot(middle[2], inverse[2])
    scale, rest, _ = mixed((middle[0], middle[1][:, :width]), inverse, square)
    root = lax.rsqrt(bound)
    columns = inv_col * rest * (jnp.sqrt(squares_row[:, :width]) * root)
    return scale * root, columns.astype(BF16)


def kernel(
    count,
    design_ref, target_ref, coeffs_ref, tau_ref, bucket_ref, sign_ref, order_ref,
    out_ref,
    piece, own, owned, partner, mine_self, mine_other, their_self, their_other,
    deal_send, deal_recv, pass_send, pass_recv, swap_send, swap_recv, gram_send, gram_recv,
):
    me = lax.axis_index("row")
    sibling = {"grp": 1 - lax.axis_index("grp")}
    depth = count.bit_length() - 1
    half = count * KB
    chunk = half // CHUNKS

    def paired(turn):
        step = 1 << (turn % depth)
        return {"row": me + step * (1 - 2 * ((me // step) % 2))}

    def remote(source, target, send, recv, device):
        return pltpu.make_async_remote_copy(
            src_ref=source, dst_ref=target, send_sem=send, recv_sem=recv,
            device_id=device, device_id_type=MESH,
        )

    parity = me % 2
    groups = count // 2
    group = me // 2

    def place(number):
        return 2 * number + parity

    peers = [{"row": place(lax.rem(group + away, groups))} for away in range(1, groups)]
    peers += [paired(0), sibling]
    barrier = pltpu.get_barrier_semaphore()
    for peer in peers:
        pl.semaphore_signal(barrier, inc=1, device_id=peer, device_id_type=MESH)

    rows = design_ref.shape[0]
    fitted = lax.dot_general(
        jnp.broadcast_to(coeffs_ref[...], (16, coeffs_ref.shape[1])),
        design_ref[...],
        (((1,), (1,)), ((), ())),
        preferred_element_type=F32,
    )[:1]
    residual = target_ref[...] - fitted
    blocks = tau_ref.shape[0]
    lane = lax.broadcasted_iota(jnp.int32, (1, rows), 1)
    level = jnp.zeros((1, rows), F32)
    for block in range(blocks):
        first = block * (rows // blocks)
        level = jnp.where(lane >= first, tau_ref[block].astype(F32), level)
    quantile = 0.1 + 0.25 * level
    upper = jax.nn.sigmoid(residual / 0.2)
    weight = (quantile * upper + (1.0 - quantile) * (1.0 - upper)) / jnp.sqrt(
        residual * residual + 0.25
    )
    signed = (2.0 * sign_ref[...].astype(F32) - 1.0) * jnp.sqrt(weight)
    slots = lax.broadcasted_iota(jnp.int32, (KB, rows), 0)
    embed = jnp.where(slots == bucket_ref[...], signed, 0.0).astype(BF16)

    sketch = dot(embed, design_ref[...])

    def sketch_of(position):
        wanted = jnp.full((KB, PANEL), order_ref[position], jnp.int32)
        chosen = sketch[:, :PANEL]
        for panel in range(1, sketch.shape[1] // PANEL):
            chosen = jnp.where(
                wanted == panel, sketch[:, panel * PANEL : (panel + 1) * PANEL], chosen
            )
        return chosen.astype(BF16)

    def rows_of(source):
        return pl.ds(pl.multiple_of(source * KB, KB), KB)

    pl.semaphore_wait(barrier, len(peers))

    first = (owned, partner)

    def deal(away, side, source, device):
        return remote(
            piece.at[away, side], first[side].at[0, rows_of(source)],
            deal_send.at[away, side], deal_recv.at[source // 2, side], device,
        )

    for away in range(1, groups):
        position = place(lax.rem(group + away, groups))
        for side in range(2):
            piece[away, side] = sketch_of(position + side * (1 - 2 * parity))
            deal(away, side, me, {"row": position}).start()
    for side in range(2):
        first[side][0, rows_of(me), :] = sketch_of(me + side * (1 - 2 * parity))

    def passed(source, side):
        return remote(
            first[side].at[0, rows_of(source)], first[1 - side].at[0, rows_of(source)],
            pass_send.at[source // 2, side], pass_recv.at[source // 2, side], paired(0),
        )

    def arrived(number, side):
        source = 2 * number + 1 - parity
        return remote(
            first[1 - side].at[0, rows_of(source)], first[side].at[0, rows_of(source)],
            pass_send.at[number, 1 - side], pass_recv.at[number, 1 - side], paired(0),
        )

    for side in range(2):
        passed(me, side).start()
    for away in range(1, groups):
        source = place(lax.rem(group + groups - away, groups))
        for side in range(2):
            deal(away, side, source, {"row": source}).wait_recv()
            passed(source, side).start()

    def swap(turn, index):
        part = pl.ds(index * chunk, chunk)
        return remote(
            owned.at[turn, part], partner.at[turn, part],
            swap_send.at[turn, index], swap_recv.at[turn, index], paired(turn),
        )

    def self_copy(turn):
        return remote(
            mine_self.at[turn], their_self.at[turn], gram_send.at[turn, 0],
            gram_recv.at[turn, 0], sibling,
        )

    def other_copy(turn):
        return remote(
            mine_other.at[turn], their_other.at[turn], gram_send.at[turn, 1],
            gram_recv.at[turn, 1], sibling,
        )

    for turn in range(ROUNDS):
        if turn > 0:
            held = owned[turn]
            mine_self[turn] = cross(held, held)
            self_copy(turn).start()
        if turn == 0:
            for number in range(groups):
                for side in range(2):
                    arrived(number, side).wait_recv()
        else:
            for index in range(CHUNKS):
                swap(turn, index).wait_recv()
        if turn == 0:
            held = owned[turn]
            mine_self[turn] = cross(held, held)
            self_copy(turn).start()
        both = jnp.concatenate([held, partner[turn]], axis=1)
        mine_other[turn] = cross(partner[turn], both)
        other_copy(turn).start()
        self_copy(turn).wait_recv()
        self_gram = mine_self[turn] + their_self[turn]
        other_copy(turn).wait_recv()
        other_gram = mine_other[turn] + their_other[turn]
        gram = jnp.concatenate(
            [
                jnp.concatenate([self_gram, other_gram[:, :PANEL].T], axis=1),
                other_gram,
            ],
            axis=0,
        )
        scale, mixing = transform_columns(gram, PANEL)
        for index in range(CHUNKS):
            part = pl.ds(index * chunk, chunk)
            mine = owned[turn, part, :]
            kept = own[part, :] if turn > 0 else mine.astype(F32)
            fresh = scale * kept + dot(
                jnp.concatenate([mine, partner[turn, part, :]], axis=1), mixing
            )
            if turn < ROUNDS - 1:
                own[part, :] = fresh
                owned[turn + 1, part, :] = fresh.astype(BF16)
                swap(turn + 1, index).start()
            else:
                out_ref[part, :] = fresh

    for side in range(2):
        for away in range(1, groups):
            deal(away, side, me, {"row": place(lax.rem(group + away, groups))}).wait_send()
        for number in range(groups):
            passed(place(number), side).wait_send()
    for turn in range(ROUNDS):
        self_copy(turn).wait_send()
        other_copy(turn).wait_send()
        if turn > 0:
            for index in range(CHUNKS):
                swap(turn, index).wait_send()


def per_device(count, design, target, coeffs, tau_level, bucket, sign_bit, panel_order):
    half = count * KB
    vmem = pl.BlockSpec(memory_space=pltpu.VMEM)
    smem = pl.BlockSpec(memory_space=pltpu.SMEM)
    dma = pltpu.SemaphoreType.DMA
    return pl.pallas_call(
        functools.partial(kernel, count),
        out_shape=jax.ShapeDtypeStruct((half, PANEL), F32),
        in_specs=[vmem, vmem, vmem, smem, vmem, vmem, smem],
        out_specs=vmem,
        scratch_shapes=[
            pltpu.VMEM((count // 2, 2, KB, PANEL), BF16),
            pltpu.VMEM((half, PANEL), F32),
            pltpu.VMEM((ROUNDS, half, PANEL), BF16),
            pltpu.VMEM((ROUNDS, half, PANEL), BF16),
            pltpu.VMEM((ROUNDS, PANEL, PANEL), F32),
            pltpu.VMEM((ROUNDS, PANEL, 2 * PANEL), F32),
            pltpu.VMEM((ROUNDS, PANEL, PANEL), F32),
            pltpu.VMEM((ROUNDS, PANEL, 2 * PANEL), F32),
            *[dma((count // 2, 2))] * 4,
            dma((ROUNDS, CHUNKS)), dma((ROUNDS, CHUNKS)), dma((ROUNDS, 2)), dma((ROUNDS, 2)),
        ],
        compiler_params=pltpu.CompilerParams(
            collective_id=0, has_side_effects=True, vmem_limit_bytes=48 * 2**20
        ),
    )(
        design, target.reshape(1, -1), coeffs.reshape(1, -1), tau_level,
        bucket.reshape(1, -1), sign_bit.reshape(1, -1), panel_order,
    )


def solution(mesh):
    placed = (
        P(("parts", "grp", "row"), None),
        P(("parts", "grp", "row")),
        P("parts"),
        P(("parts", "grp", "row")),
        P(("parts", "grp", "row")),
        P(("parts", "grp", "row")),
        P("parts"),
    )
    return jax.shard_map(
        functools.partial(per_device, mesh.shape["row"]),
        mesh=mesh,
        in_specs=placed,
        out_specs=P(("parts", "grp"), "row"),
        check_vma=False,
    )
```

```python
import functools

import jax
import jax.numpy as jnp
from jax import lax
from jax.experimental import pallas as pl
from jax.experimental.pallas import tpu as pltpu
from jax.sharding import PartitionSpec as P

PANEL = 128
KB = 64
ROUNDS = 5
NS_ITERS = 4
CHUNKS = 2
MESH = pl.DeviceIdType.MESH
F32 = jnp.float32
BF16 = jnp.bfloat16


def dot(left, right):
    return jnp.dot(left, right, preferred_element_type=F32)


def cross(left, right):
    return lax.dot_general(left, right, (((0,), (0,)), ((), ())), preferred_element_type=F32)


def shifted(scale, rest):
    return scale, rest, rest.astype(BF16)


def mixed(left, right, square):
    return shifted(left[0] * right[0], right[0] * left[1] + left[0] * right[1] + square)


def product(left, right):
    return mixed(left, right, dot(left[2], right[2]))


def middle_of(value):
    return shifted(1.5 - 0.5 * value[0], -0.5 * value[1])


def transform_columns(gram, width):
    size = gram.shape[0]
    same = lax.broadcasted_iota(jnp.int32, gram.shape, 0) == lax.broadcasted_iota(
        jnp.int32, gram.shape, 1
    )
    diagonal = jnp.where(same, gram, 0.0)
    squares_row = jnp.sum(diagonal, axis=0, keepdims=True)
    squares_col = jnp.sum(diagonal, axis=1, keepdims=True)
    inv_row = lax.rsqrt(squares_row)
    inv_col = lax.rsqrt(squares_col)
    normed = gram * inv_col * inv_row
    bound = jnp.max(jnp.sum(jnp.abs(normed), axis=0, keepdims=True), axis=1, keepdims=True)
    share = 1.0 / bound
    current = shifted(share, normed * share - jnp.where(same, share, 0.0))
    middle = middle_of(current)
    inverse = middle
    current = product(current, middle)
    for iteration in range(1, NS_ITERS):
        middle = middle_of(product(inverse, current))
        if iteration < NS_ITERS - 1:
            squares = dot(jnp.concatenate([current[2], inverse[2]], axis=0), middle[2])
            current = mixed(current, middle, squares[:size])
            inverse = mixed(inverse, middle, squares[size:])
    inverse = tuple([inverse[0]] + [part[:, :width] for part in inverse[1:]])
    square = dot(middle[2], inverse[2])
    scale, rest, _ = mixed((middle[0], middle[1][:, :width]), inverse, square)
    root = lax.rsqrt(bound)
    columns = inv_col * rest * (jnp.sqrt(squares_row[:, :width]) * root)
    return scale * root, columns.astype(BF16)


def kernel(
    count,
    design_ref, target_ref, coeffs_ref, tau_ref, bucket_ref, sign_ref, order_ref,
    out_ref,
    piece, own, owned, partner, mine_gram, their_gram,
    deal_send, deal_recv, pass_send, pass_recv, swap_send, swap_recv, gram_send, gram_recv,
):
    me = lax.axis_index("row")
    sibling = {"grp": 1 - lax.axis_index("grp")}
    depth = count.bit_length() - 1
    half = count * KB
    chunk = half // CHUNKS

    def paired(turn):
        step = 1 << (turn % depth)
        return {"row": me + step * (1 - 2 * ((me // step) % 2))}

    def remote(source, target, send, recv, device):
        return pltpu.make_async_remote_copy(
            src_ref=source, dst_ref=target, send_sem=send, recv_sem=recv,
            device_id=device, device_id_type=MESH,
        )

    parity = me % 2
    groups = count // 2
    group = me // 2

    def place(number):
        return 2 * number + parity

    peers = [{"row": place(lax.rem(group + away, groups))} for away in range(1, groups)]
    peers += [paired(0), sibling]
    barrier = pltpu.get_barrier_semaphore()
    for peer in peers:
        pl.semaphore_signal(barrier, inc=1, device_id=peer, device_id_type=MESH)

    rows = design_ref.shape[0]
    fitted = lax.dot_general(
        jnp.broadcast_to(coeffs_ref[...], (16, coeffs_ref.shape[1])),
        design_ref[...],
        (((1,), (1,)), ((), ())),
        preferred_element_type=F32,
    )[:1]
    residual = target_ref[...] - fitted
    blocks = tau_ref.shape[0]
    lane = lax.broadcasted_iota(jnp.int32, (1, rows), 1)
    level = jnp.zeros((1, rows), F32)
    for block in range(blocks):
        first = block * (rows // blocks)
        level = jnp.where(lane >= first, tau_ref[block].astype(F32), level)
    quantile = 0.1 + 0.25 * level
    upper = jax.nn.sigmoid(residual / 0.2)
    weight = (quantile * upper + (1.0 - quantile) * (1.0 - upper)) / jnp.sqrt(
        residual * residual + 0.25
    )
    signed = (2.0 * sign_ref[...].astype(F32) - 1.0) * jnp.sqrt(weight)
    slots = lax.broadcasted_iota(jnp.int32, (KB, rows), 0)
    embed = jnp.where(slots == bucket_ref[...], signed, 0.0).astype(BF16)

    sketch = dot(embed, design_ref[...])

    def sketch_of(position):
        wanted = jnp.full((KB, PANEL), order_ref[position], jnp.int32)
        chosen = sketch[:, :PANEL]
        for panel in range(1, sketch.shape[1] // PANEL):
            chosen = jnp.where(
                wanted == panel, sketch[:, panel * PANEL : (panel + 1) * PANEL], chosen
            )
        return chosen.astype(BF16)

    def rows_of(source):
        return pl.ds(pl.multiple_of(source * KB, KB), KB)

    pl.semaphore_wait(barrier, len(peers))

    first = (owned, partner)

    def deal(away, side, source, device):
        return remote(
            piece.at[away, side], first[side].at[0, rows_of(source)],
            deal_send.at[away, side], deal_recv.at[source // 2, side], device,
        )

    for away in range(1, groups):
        position = place(lax.rem(group + away, groups))
        for side in range(2):
            piece[away, side] = sketch_of(position + side * (1 - 2 * parity))
            deal(away, side, me, {"row": position}).start()
    for side in range(2):
        first[side][0, rows_of(me), :] = sketch_of(me + side * (1 - 2 * parity))

    def passed(source, side):
        return remote(
            first[side].at[0, rows_of(source)], first[1 - side].at[0, rows_of(source)],
            pass_send.at[source // 2, side], pass_recv.at[source // 2, side], paired(0),
        )

    def arrived(number, side):
        source = 2 * number + 1 - parity
        return remote(
            first[1 - side].at[0, rows_of(source)], first[side].at[0, rows_of(source)],
            pass_send.at[number, 1 - side], pass_recv.at[number, 1 - side], paired(0),
        )

    for side in range(2):
        passed(me, side).start()
    for away in range(1, groups):
        source = place(lax.rem(group + groups - away, groups))
        for side in range(2):
            deal(away, side, source, {"row": source}).wait_recv()
            passed(source, side).start()

    def swap(turn, index):
        part = pl.ds(index * chunk, chunk)
        return remote(
            owned.at[turn, part], partner.at[turn, part],
            swap_send.at[turn, index], swap_recv.at[turn, index], paired(turn),
        )

    def gram_copy(turn):
        return remote(
            mine_gram.at[turn], their_gram.at[turn], gram_send.at[turn],
            gram_recv.at[turn], sibling,
        )

    for turn in range(ROUNDS):
        if turn > 0:
            held = owned[turn]
            mine_gram[turn, :, 2 * PANEL :] = cross(held, held)
        if turn == 0:
            for number in range(groups):
                for side in range(2):
                    arrived(number, side).wait_recv()
        else:
            for index in range(CHUNKS):
                swap(turn, index).wait_recv()
        if turn == 0:
            held = owned[turn]
            mine_gram[turn, :, 2 * PANEL :] = cross(held, held)
        both = jnp.concatenate([held, partner[turn]], axis=1)
        mine_gram[turn, :, : 2 * PANEL] = cross(partner[turn], both)
        gram_copy(turn).start()
        gram_copy(turn).wait_recv()
        total = mine_gram[turn] + their_gram[turn]
        other_gram = total[:, : 2 * PANEL]
        gram = jnp.concatenate(
            [
                jnp.concatenate([total[:, 2 * PANEL :], other_gram[:, :PANEL].T], axis=1),
                other_gram,
            ],
            axis=0,
        )
        scale, mixing = transform_columns(gram, PANEL)
        for index in range(CHUNKS):
            part = pl.ds(index * chunk, chunk)
            mine = owned[turn, part, :]
            kept = own[part, :] if turn > 0 else mine.astype(F32)
            fresh = scale * kept + dot(
                jnp.concatenate([mine, partner[turn, part, :]], axis=1), mixing
            )
            if turn < ROUNDS - 1:
                own[part, :] = fresh
                owned[turn + 1, part, :] = fresh.astype(BF16)
                swap(turn + 1, index).start()
            else:
                out_ref[part, :] = fresh

    for side in range(2):
        for away in range(1, groups):
            deal(away, side, me, {"row": place(lax.rem(group + away, groups))}).wait_send()
        for number in range(groups):
            passed(place(number), side).wait_send()
    for turn in range(ROUNDS):
        gram_copy(turn).wait_send()
        if turn > 0:
            for index in range(CHUNKS):
                swap(turn, index).wait_send()


def per_device(count, design, target, coeffs, tau_level, bucket, sign_bit, panel_order):
    half = count * KB
    vmem = pl.BlockSpec(memory_space=pltpu.VMEM)
    smem = pl.BlockSpec(memory_space=pltpu.SMEM)
    dma = pltpu.SemaphoreType.DMA
    return pl.pallas_call(
        functools.partial(kernel, count),
        out_shape=jax.ShapeDtypeStruct((half, PANEL), F32),
        in_specs=[vmem, vmem, vmem, smem, vmem, vmem, smem],
        out_specs=vmem,
        scratch_shapes=[
            pltpu.VMEM((count // 2, 2, KB, PANEL), BF16),
            pltpu.VMEM((half, PANEL), F32),
            pltpu.VMEM((ROUNDS, half, PANEL), BF16),
            pltpu.VMEM((ROUNDS, half, PANEL), BF16),
            pltpu.VMEM((ROUNDS, PANEL, 3 * PANEL), F32),
            pltpu.VMEM((ROUNDS, PANEL, 3 * PANEL), F32),
            *[dma((count // 2, 2))] * 4,
            dma((ROUNDS, CHUNKS)), dma((ROUNDS, CHUNKS)), dma((ROUNDS,)), dma((ROUNDS,)),
        ],
        compiler_params=pltpu.CompilerParams(
            collective_id=0, has_side_effects=True, vmem_limit_bytes=48 * 2**20
        ),
    )(
        design, target.reshape(1, -1), coeffs.reshape(1, -1), tau_level,
        bucket.reshape(1, -1), sign_bit.reshape(1, -1), panel_order,
    )


def solution(mesh):
    placed = (
        P(("parts", "grp", "row"), None),
        P(("parts", "grp", "row")),
        P("parts"),
        P(("parts", "grp", "row")),
        P(("parts", "grp", "row")),
        P(("parts", "grp", "row")),
        P("parts"),
    )
    return jax.shard_map(
        functools.partial(per_device, mesh.shape["row"]),
        mesh=mesh,
        in_specs=placed,
        out_specs=P(("parts", "grp"), "row"),
        check_vma=False,
    )
```
